256 devices in a mesh: rows: 32 (over y_lo, z, core), pairs: 8 (over x, y_hi).
Axes of the slice: x: 4, y: 4 (y_hi: 2, y_lo: 2; y = y_hi * 2 + y_lo), z: 8, core: 2. Of those that a mesh axis runs over, the one named last changes fastest.
Arguments:
- snapshots: float32 [131072, 1024], P('rows', 'pairs'), may hold values from -40 to 40
Outputs:
- rotated_out: float32 [131072, 1024], P('rows', 'pairs')
- column_norms: float32 [1024], P('pairs')
The draws below stay inside these ranges and needn't reach their ends.
All inputs are finite; a program needn't handle non-finite values.
Results may differ from the reference program's by a relative error of at most 0.0003.
Values sent between devices are 32-bit elements; how exact they have to be, the bound alone decides.
No kernel may reach another device: no remote copies, remote signals or barrier semaphores. Data moves between devices by JAX's collectives and lax.ppermute only.
A program may use at most 64 MiB of HBM per device.

```python
import math
import jax
import jax.numpy as jnp
from jax import lax

BS = 64
STEPS = 6
ROWS = 131072
COLS = 1024
N_PAIRS = 8


def draw_snapshots(key, part):
    key = jax.random.fold_in(key, 11)
    keys = jax.random.split(key, 5)
    scales = jnp.exp(jax.random.uniform(keys[0], (1, COLS), jnp.float32, math.log(0.3), math.log(3.0)))
    weights = jax.random.normal(keys[1], (1, COLS), jnp.float32)
    noise = jax.random.normal(keys[2], (ROWS, COLS), jnp.float32)
    shared = 0.3 * jax.random.normal(keys[3], (ROWS, 1), jnp.float32)
    rowscale = jnp.exp(jax.random.uniform(keys[4], (ROWS, 1), jnp.float32, math.log(0.5), math.log(2.0)))
    values = scales * rowscale * (noise + shared * weights)
    return jnp.clip(values, -40.0, 40.0)


def setup_inputs(seed: int = 0) -> dict:
    key_list = jax.random.split(jax.random.key(seed), 2)
    snapshots = draw_snapshots(jax.random.fold_in(key_list[1], 71), 0)
    return dict(snapshots=snapshots)


HIGH = lax.Precision.HIGHEST

def rotation(gram):
    size = gram.shape[0]
    diag = jnp.diagonal(gram)
    ratio = gram / (diag[:, None] + diag[None, :])
    row_ids = lax.broadcasted_iota(jnp.int32, (size, size), 0)
    col_ids = lax.broadcasted_iota(jnp.int32, (size, size), 1)
    upper = jnp.where(col_ids > row_ids, ratio, jnp.zeros_like(ratio))
    skew = 0.5 * (upper - upper.T)
    eye = jnp.eye(size, dtype=gram.dtype)
    plus = eye + skew
    system = eye - jnp.dot(skew, skew, precision=HIGH)
    factor = jnp.linalg.cholesky(system)
    right = jnp.dot(plus, plus, precision=HIGH)
    inner = jax.scipy.linalg.solve_triangular(factor, right, lower=True)
    return jax.scipy.linalg.solve_triangular(factor, inner, lower=True, trans=1)

def shuffle(top, bottom, axis, pairs):
    first_top = lax.slice_in_dim(top, 0, 1, axis=axis)
    first_bottom = lax.slice_in_dim(bottom, 0, 1, axis=axis)
    middle_top = lax.slice_in_dim(top, 0, pairs - 1, axis=axis)
    rest_bottom = lax.slice_in_dim(bottom, 1, pairs, axis=axis)
    last_top = lax.slice_in_dim(top, pairs - 1, pairs, axis=axis)
    new_top = jnp.concatenate([first_top, first_bottom, lax.slice_in_dim(middle_top, 1, pairs - 1, axis=axis)], axis=axis)
    new_bottom = jnp.concatenate([rest_bottom, last_top], axis=axis)
    return (new_top, new_bottom)

def reference(snapshots):
    pairs = N_PAIRS
    width = BS
    data = snapshots.reshape(ROWS, pairs, 2 * width)
    norms = jnp.zeros((pairs, 2 * width), jnp.float32)
    for step in range(STEPS):
        gram = jnp.einsum('rka,rkb->kab', data, data, precision=HIGH)
        turn = jax.vmap(rotation)(gram)
        data = jnp.einsum('rka,kab->rkb', data, turn, precision=HIGH)
        image = jnp.einsum('kab,kbc->kac', gram, turn, precision=HIGH)
        norms = jnp.sqrt(lax.optimization_barrier(jnp.sum(turn * image, axis=1)))
        new_top, new_bottom = shuffle(data[:, :, :width], data[:, :, width:], 1, pairs)
        data = jnp.concatenate([new_top, new_bottom], axis=2)
        norm_top, norm_bottom = shuffle(norms[:, :width], norms[:, width:], 0, pairs)
        norms = jnp.concatenate([norm_top, norm_bottom], axis=1)
    return (data.reshape(ROWS, COLS), norms.reshape(COLS))
```

```python
import jax
import jax.numpy as jnp
import numpy as np
from jax import lax
from jax.experimental import pallas as pl
from jax.experimental.pallas import tpu as pltpu
from jax.sharding import PartitionSpec as P

STEPS = 6
HALF = 64
WIDE = 2 * HALF
PAIRS = 8
BLOCKS = [(i, j) for i in range(PAIRS) for j in range(i, PAIRS)]
INDEX = {block: t for t, block in enumerate(BLOCKS)}
SHARE = len(BLOCKS) // 2

PAIR_AXES = ("x", "yh")
SUM_AXES = ("yl", "z", "x", "yh")
F32 = jnp.float32
BF16 = jnp.bfloat16
VMEM_LIMIT = 60 * 1024 * 1024

MOVED = {0: 0, 1: 2, 2 * PAIRS - 2: 2 * PAIRS - 1}
for place in range(1, PAIRS - 1):
    MOVED[2 * place] = 2 * (place + 1)
for place in range(1, PAIRS):
    MOVED[2 * place + 1] = 2 * (place - 1) + 1


def split(x):
    high = x.astype(BF16)
    low = (x - high.astype(F32)).astype(BF16)
    return high, low


def left(x):
    return jnp.concatenate(split(x), axis=1)


def right(x):
    both = jnp.concatenate(split(x), axis=1)
    return jnp.concatenate([both, both], axis=0)


def mul(a, b):
    y = jnp.dot(a, b, preferred_element_type=F32)
    n = y.shape[1] // 2
    return y[:, :n] + y[:, n:]


def gram_kernel(x_ref, keep_ref, send_ref, lhs, rhs):
    core = lax.axis_index("c")
    for k in range(PAIRS):
        x = x_ref[k]
        rhs[k] = jnp.concatenate(split(x), axis=1)
        lhs[k] = jnp.concatenate(split(x.T), axis=0)
    for t, (i, j) in enumerate(BLOCKS):
        y = jnp.dot(lhs[i], rhs[j], preferred_element_type=F32)
        y = y[:WIDE] + y[WIDE:]
        y = y[:, :WIDE] + y[:, WIDE:]
        mine = core == t // SHARE

        @pl.when(mine)
        def _():
            keep_ref[t % SHARE] = y

        @pl.when(jnp.logical_not(mine))
        def _():
            send_ref[t % SHARE] = y


def chain_kernel(mine_ref, other_ref, x_ref, y_ref, norms_ref, gram, data, skew, inv, power, turn, turned, norms):
    core = lax.axis_index("c")
    position = lax.axis_index("x") * 2 + lax.axis_index("yh")
    row = lax.broadcasted_iota(jnp.int32, (WIDE, WIDE), 0)
    col = lax.broadcasted_iota(jnp.int32, (WIDE, WIDE), 1)
    eye = (row == col).astype(F32)
    for t in range(len(BLOCKS)):
        gram[0, t] = jnp.where(core == t // SHARE, mine_ref[t % SHARE], other_ref[t % SHARE])
    for k in range(PAIRS):
        data[0, k] = x_ref[k]

    def rotations(now):
        radius = jnp.zeros((1, 1), F32)
        for k in range(PAIRS):
            g = gram[now, INDEX[k, k]]
            diag = g * eye
            total = jnp.sum(diag, axis=0, keepdims=True) + jnp.sum(diag, axis=1, keepdims=True)
            ratio = jnp.clip(0.5 * (g / total), -0.25, 0.25)
            s = jnp.where(col > row, ratio, jnp.where(col < row, -ratio, 0.0))
            skew[k] = s
            square = mul(left(s), right(s))
            bound = jnp.sqrt(0.5 * jnp.sum(square * square, axis=(0, 1), keepdims=True)) * 1.001
            scale = 2.0 / (2.0 + bound)
            power[k] = (1.0 - scale) * eye + scale * square
            inv[k] = scale * (eye + s)
            radius = jnp.maximum(radius, bound / (2.0 + bound))

        def multiply_on(rate):
            for k in range(PAIRS):
                p = inv[k]
                r = power[k]
                y = mul(jnp.concatenate([left(p), left(r)], axis=0), right(r))
                inv[k] = p + y[:WIDE]
                power[k] = y[WIDE:]
            return rate * rate

        lax.while_loop(lambda rate: rate > 5e-5, multiply_on, radius[0, 0])

        def correct(carry):
            rounds, _ = carry
            worst = jnp.zeros((1, 1), F32)
            for k in range(PAIRS):
                p = inv[k]
                e = eye - p + mul(left(skew[k]), right(p))
                inv[k] = p + mul(left(p), right(e))
                worst = jnp.maximum(worst, jnp.sum(e * e, axis=(0, 1), keepdims=True))
            return rounds + 1, worst[0, 0]

        lax.while_loop(lambda c: jnp.logical_and(c[1] > 1e-6, c[0] < 40), correct, (0, jnp.float32(1.0)))

        for k in range(PAIRS):
            j = 2.0 * inv[k] - eye
            turn[k] = right(j)
            turned[k] = left(j.T)

    def put(ref, lead, value, a, b, to_a, to_b):
        part = value[a * HALF : (a + 1) * HALF, :]
        if b != to_b:
            part = pltpu.roll(part, HALF, 1)
        ref[lead + (pl.ds(to_a * HALF, HALF), pl.ds(to_b * HALF, HALF))] = part[:, to_b * HALF : (to_b + 1) * HALF]

    def rotate_gram(now, later):
        for i, j in BLOCKS:
            h = mul(left(gram[now, INDEX[i, j]]), turn[j])
            g = mul(turned[i], right(h))
            flipped = None
            for a in range(2):
                for b in range(2):
                    to_i, to_j = MOVED[2 * i + a], MOVED[2 * j + b]
                    if i == j and a != b and to_i > to_j:
                        continue
                    if to_i <= to_j:
                        put(gram, (later, INDEX[to_i // 2, to_j // 2]), g, a, b, to_i % 2, to_j % 2)
                    if to_i > to_j or (to_i != to_j and to_i // 2 == to_j // 2):
                        if flipped is None:
                            flipped = g.T
                        if to_i > to_j and to_i // 2 != to_j // 2:
                            put(gram, (later, INDEX[to_j // 2, to_i // 2]), flipped, b, a, to_j % 2, to_i % 2)
                        elif to_i > to_j:
                            put(gram, (later, INDEX[to_j // 2, to_i // 2]), flipped, b, a, to_j % 2, to_i % 2)
                            put(gram, (later, INDEX[to_j // 2, to_i // 2]), g, a, b, to_i % 2, to_j % 2)
                        else:
                            put(gram, (later, INDEX[to_i // 2, to_j // 2]), flipped, b, a, to_j % 2, to_i % 2)

    def rotate_data(now, ref, lead):
        for k in range(PAIRS):
            y = mul(left(data[now, k]), turn[k])
            for b in range(2):
                to = MOVED[2 * k + b]
                part = y if b == to % 2 else pltpu.roll(y, HALF, 1)
                side = to % 2 * HALF
                ref[lead + (to // 2, slice(None), pl.ds(side, HALF))] = part[:, side : side + HALF]

    def step(s, carry):
        now = lax.rem(s, 2)
        later = 1 - now
        rotations(now)
        rotate_gram(now, later)
        rotate_data(now, data, (later,))
        return carry

    lax.fori_loop(0, STEPS - 1, step, 0)
    now = (STEPS - 1) % 2
    rotations(now)
    rotate_data(now, y_ref, ())
    for k in range(PAIRS):
        j = 2.0 * inv[k] - eye
        h = mul(left(gram[now, INDEX[k, k]]), turn[k])
        n = jnp.sqrt(jnp.maximum(jnp.sum(j * h, axis=0, keepdims=True), 0.0))
        for b in range(2):
            to = MOVED[2 * k + b]
            part = n if b == to % 2 else pltpu.roll(n, HALF, 1)
            side = to % 2 * HALF
            norms[to // 2, :, pl.ds(side, HALF)] = part[:, side : side + HALF]
    norms_ref[...] = norms[position]


def local_gram(x):
    rows = x.shape[1]
    out = jax.ShapeDtypeStruct((SHARE, WIDE, WIDE), F32)
    return pl.pallas_call(
        gram_kernel,
        out_shape=(out, out),
        scratch_shapes=[
            pltpu.VMEM((PAIRS, 2 * WIDE, rows), BF16),
            pltpu.VMEM((PAIRS, rows, 2 * WIDE), BF16),
        ],
        compiler_params=pltpu.CompilerParams(vmem_limit_bytes=VMEM_LIMIT),
        name="gram",
    )(x)


def chain(mine, other, x):
    rows = x.shape[1]
    square = pltpu.VMEM((PAIRS, WIDE, WIDE), F32)
    return pl.pallas_call(
        chain_kernel,
        out_shape=(
            jax.ShapeDtypeStruct((PAIRS, rows, WIDE), F32),
            jax.ShapeDtypeStruct((1, WIDE), F32),
        ),
        scratch_shapes=[
            pltpu.VMEM((2, len(BLOCKS), WIDE, WIDE), F32),
            pltpu.VMEM((2, PAIRS, rows, WIDE), F32),
            square,
            square,
            square,
            pltpu.VMEM((PAIRS, 2 * WIDE, 2 * WIDE), BF16),
            pltpu.VMEM((PAIRS, WIDE, 2 * WIDE), BF16),
            pltpu.VMEM((PAIRS, 1, WIDE), F32),
        ],
        compiler_params=pltpu.CompilerParams(vmem_limit_bytes=VMEM_LIMIT),
        name="chain",
    )(mine, other, x)


def body(snapshots):
    rows = snapshots.shape[0] // PAIRS
    sharers = lax.axis_size(SUM_AXES)
    x = lax.all_to_all(snapshots, PAIR_AXES, 0, 0, tiled=True).reshape(PAIRS, rows, WIDE)
    keep, send = local_gram(x)
    got = lax.ppermute(send, "c", [(0, 1), (1, 0)])
    part = (keep + got).reshape(sharers, 1, -1)
    part = jnp.sum(lax.all_to_all(part, SUM_AXES, 0, 0, tiled=True), axis=0, keepdims=True)
    part = jnp.broadcast_to(part, (sharers, 1, part.shape[2]))
    mine = lax.all_to_all(part, SUM_AXES, 0, 0, tiled=True).reshape(SHARE, WIDE, WIDE)
    other = lax.ppermute(mine, "c", [(0, 1), (1, 0)])
    y, norms = chain(mine, other, x)
    out = lax.all_to_all(y.reshape(snapshots.shape), PAIR_AXES, 0, 0, tiled=True)
    return out, norms.reshape(WIDE)


def solution(mesh):
    axes = ("yl", "z", "c", "x", "yh")
    finer = jax.sharding.Mesh(mesh.devices.reshape(2, 8, 2, 4, 2), axes)
    rows, pairs = ("yl", "z", "c"), PAIR_AXES
    return jax.shard_map(
        body,
        mesh=finer,
        in_specs=(P(rows, pairs),),
        out_specs=(P(rows, pairs), P(pairs)),
        check_vma=False,
    )
```

```python
import jax
import jax.numpy as jnp
import numpy as np
from jax import lax
from jax.experimental import pallas as pl
from jax.experimental.pallas import tpu as pltpu
from jax.sharding import PartitionSpec as P

STEPS = 6
HALF = 64
WIDE = 2 * HALF
PAIRS = 8
BLOCKS = [(i, j) for i in range(PAIRS) for j in range(i, PAIRS)]
INDEX = {block: t for t, block in enumerate(BLOCKS)}
SHARE = len(BLOCKS) // 2

PAIR_AXES = ("x", "yh")
SUM_AXES = ("yl", "z", "x", "yh")
F32 = jnp.float32
BF16 = jnp.bfloat16
VMEM_LIMIT = 60 * 1024 * 1024

MOVED = {0: 0, 1: 2, 2 * PAIRS - 2: 2 * PAIRS - 1}
for place in range(1, PAIRS - 1):
    MOVED[2 * place] = 2 * (place + 1)
for place in range(1, PAIRS):
    MOVED[2 * place + 1] = 2 * (place - 1) + 1


def sources(block):
    return [next(t for t, u in MOVED.items() if u == b) for b in block]


def updates():
    lists = []
    needed = {(2 * k + a, 2 * k + b) for k in range(PAIRS) for a in range(2) for b in range(a, 2)}
    inside = set(needed)
    for _ in range(STEPS - 1):
        blocks = set()
        for block in needed:
            old = sorted(sources(block))
            blocks.add((old[0] // 2, old[1] // 2))
        lists.insert(0, sorted(blocks))
        needed = set(inside)
        for i, j in blocks:
            needed |= {tuple(sorted((2 * i + a, 2 * j + b))) for a in range(2) for b in range(2)}
    return lists


KMODE = True


def split(x):
    high = x.astype(BF16)
    low = (x - high.astype(F32)).astype(BF16)
    return high, low


def left(x, k=None):
    return jnp.concatenate(split(x), axis=1 if (KMODE if k is None else k) else 0)


def right(x, k=None):
    both = jnp.concatenate(split(x), axis=1)
    return jnp.concatenate([both, both], axis=0) if (KMODE if k is None else k) else both


def mul(a, b, k=None):
    y = jnp.dot(a, b, preferred_element_type=F32)
    if not (KMODE if k is None else k):
        m = y.shape[0] // 2
        y = y[:m] + y[m:]
    n = y.shape[1] // 2
    return y[:, :n] + y[:, n:]


def gram_kernel(x_ref, keep_ref, send_ref, lhs, rhs):
    core = lax.axis_index("c")
    for k in range(PAIRS):
        x = x_ref[k]
        rhs[k] = jnp.concatenate(split(x), axis=1)
        lhs[k] = jnp.concatenate(split(x.T), axis=0)

    def block(i, j):
        y = jnp.dot(lhs[i], rhs[j], preferred_element_type=F32)
        y = y[:WIDE] + y[WIDE:]
        return y[:, :WIDE] + y[:, WIDE:]

    for t in range(SHARE):
        first = block(*BLOCKS[t])
        second = block(*BLOCKS[t + SHARE])
        keep_ref[t] = jnp.where(core == 0, first, second)
        send_ref[t] = jnp.where(core == 0, second, first)


def chain_kernel(mine_ref, other_ref, x_ref, y_ref, norms_ref, gram, half, data, data_left, skew, inv, power, turn, turned, norms):
    core = lax.axis_index("c")
    position = lax.axis_index("x") * 2 + lax.axis_index("yh")
    row = lax.broadcasted_iota(jnp.int32, (WIDE, WIDE), 0)
    col = lax.broadcasted_iota(jnp.int32, (WIDE, WIDE), 1)
    eye = (row == col).astype(F32)
    for t in range(len(BLOCKS)):
        gram[t] = jnp.where(core == t // SHARE, mine_ref[t % SHARE], other_ref[t % SHARE])

    def rotations():
        radius = jnp.zeros((1, 1), F32)
        for k in range(PAIRS):
            g = gram[INDEX[k, k]]
            diag = g * eye
            total = jnp.sum(diag, axis=0, keepdims=True) + jnp.sum(diag, axis=1, keepdims=True)
            ratio = jnp.clip(0.5 * (g / total), -0.25, 0.25)
            s = jnp.where(col > row, ratio, jnp.where(col < row, -ratio, 0.0))
            skew[k] = s
            square = mul(left(s), right(s))
            bound = jnp.sqrt(0.5 * jnp.sum(square * square, axis=(0, 1), keepdims=True)) * 1.001
            scale = 2.0 / (2.0 + bound)
            power[k] = (1.0 - scale) * eye + scale * square
            inv[k] = scale * (eye + s)
            radius = jnp.maximum(radius, bound / (2.0 + bound))

        def multiply_on(rate):
            for k in range(PAIRS):
                p = inv[k]
                r = power[k]
                y = mul(jnp.concatenate([left(p, True), left(r, True)], axis=0), right(r, True), True)
                inv[k] = p + y[:WIDE]
                power[k] = y[WIDE:]
            return rate * rate

        lax.while_loop(lambda rate: rate > 2e-3, multiply_on, radius[0, 0])

        def correct(carry):
            rounds, _ = carry
            worst = jnp.zeros((1, 1), F32)
            for k in range(PAIRS):
                p = inv[k]
                e = eye - p + mul(left(skew[k]), right(p))
                inv[k] = p + mul(left(p), right(e))
                worst = jnp.maximum(worst, jnp.sum(e * e, axis=(0, 1), keepdims=True))
            return rounds + 1, worst[0, 0]

        lax.while_loop(lambda c: jnp.logical_and(c[1] > 3e-5, c[0] < 40), correct, (0, jnp.float32(1.0)))

        for k in range(PAIRS):
            j = 2.0 * inv[k] - eye
            turn[k] = right(j)
            turned[k] = left(j.T)

    def put(ref, lead, value, a, b, to_a, to_b):
        part = value[a * HALF : (a + 1) * HALF, :]
        if b != to_b:
            part = pltpu.roll(part, HALF, 1)
        ref[lead, pl.ds(to_a * HALF, HALF), pl.ds(to_b * HALF, HALF)] = part[:, to_b * HALF : (to_b + 1) * HALF]

    def rotate_gram(blocks):
        for i, j in blocks:
            half[INDEX[i, j]] = right(mul(left(gram[INDEX[i, j]]), turn[j]), False)
        for i, j in blocks:
            h = half[INDEX[i, j]]
            g = mul(turned[i], jnp.concatenate([h, h], axis=0) if KMODE else h)
            flipped = None
            for a in range(2):
                for b in range(2):
                    to_i, to_j = MOVED[2 * i + a], MOVED[2 * j + b]
                    if i == j and a != b and to_i > to_j:
                        continue
                    low, high = min(to_i, to_j), max(to_i, to_j)
                    target = INDEX[low // 2, high // 2]
                    within = low // 2 == high // 2 and low != high
                    if to_i <= to_j or within:
                        put(gram, target, g, a, b, to_i % 2, to_j % 2)
                    if to_i > to_j or within:
                        flipped = g.T if flipped is None else flipped
                        put(gram, target, flipped, b, a, to_j % 2, to_i % 2)

    def moved(k, top, bottom):
        sides = []
        for side in range(2):
            (source,) = sources([2 * k + side])
            value = data[source // 2]
            sides.append(value if source % 2 == side else pltpu.roll(value, HALF, 1))
        lane = lax.broadcasted_iota(jnp.int32, sides[0].shape, 1)
        return jnp.where(lane < HALF, sides[0], sides[1])

    def rotate_data(s):
        @pl.when(s == 0)
        def _():
            for k in range(PAIRS):
                data_left[k] = left(x_ref[k])

        @pl.when(s > 0)
        def _():
            for k in range(PAIRS):
                data_left[k] = left(moved(k, 0, 0))

        for k in range(PAIRS):
            data[k] = mul(data_left[k], turn[k])

    lists = updates()

    def step(s, carry):
        rotations()
        for first in range(STEPS - 1):
            if first and lists[first] == lists[first - 1]:
                continue
            steps = [t for t in range(STEPS - 1) if lists[t] == lists[first]]

            @pl.when(jnp.logical_and(s >= steps[0], s <= steps[-1]))
            def _():
                rotate_gram(lists[first])

        rotate_data(s)
        return carry

    lax.fori_loop(0, STEPS, step, 0)
    for k in range(PAIRS):
        y_ref[k] = moved(k, 0, 0)
    for k in range(PAIRS):
        j = 2.0 * inv[k] - eye
        h = mul(left(gram[INDEX[k, k]]), turn[k])
        n = jnp.sqrt(jnp.maximum(jnp.sum(j * h, axis=0, keepdims=True), 0.0))
        for b in range(2):
            to = MOVED[2 * k + b]
            part = n if b == to % 2 else pltpu.roll(n, HALF, 1)
            side = to % 2 * HALF
            norms[to // 2, :, pl.ds(side, HALF)] = part[:, side : side + HALF]
    norms_ref[...] = norms[position]


def local_gram(x):
    rows = x.shape[1]
    out = jax.ShapeDtypeStruct((SHARE, WIDE, WIDE), F32)
    return pl.pallas_call(
        gram_kernel,
        out_shape=(out, out),
        scratch_shapes=[
            pltpu.VMEM((PAIRS, 2 * WIDE, rows), BF16),
            pltpu.VMEM((PAIRS, rows, 2 * WIDE), BF16),
        ],
        compiler_params=pltpu.CompilerParams(vmem_limit_bytes=VMEM_LIMIT),
        name="gram",
    )(x)


def chain(mine, other, x):
    rows = x.shape[1]
    square = pltpu.VMEM((PAIRS, WIDE, WIDE), F32)
    return pl.pallas_call(
        chain_kernel,
        out_shape=(
            jax.ShapeDtypeStruct((PAIRS, rows, WIDE), F32),
            jax.ShapeDtypeStruct((1, WIDE), F32),
        ),
        scratch_shapes=[
            pltpu.VMEM((len(BLOCKS), WIDE, WIDE), F32),
            pltpu.VMEM((len(BLOCKS), WIDE, 2 * WIDE), BF16),
            pltpu.VMEM((PAIRS, rows, WIDE), F32),
            pltpu.VMEM((PAIRS, rows, 2 * WIDE) if KMODE else (PAIRS, 2 * rows, WIDE), BF16),
            square,
            square,
            square,
            pltpu.VMEM((PAIRS, 2 * WIDE, 2 * WIDE) if KMODE else (PAIRS, WIDE, 2 * WIDE), BF16),
            pltpu.VMEM((PAIRS, WIDE, 2 * WIDE) if KMODE else (PAIRS, 2 * WIDE, WIDE), BF16),
            pltpu.VMEM((PAIRS, 1, WIDE), F32),
        ],
        compiler_params=pltpu.CompilerParams(vmem_limit_bytes=VMEM_LIMIT),
        name="chain",
    )(mine, other, x)


def body(snapshots):
    rows = snapshots.shape[0] // PAIRS
    sharers = lax.axis_size(SUM_AXES)
    x = lax.all_to_all(snapshots, PAIR_AXES, 0, 0, tiled=True).reshape(PAIRS, rows, WIDE)
    keep, send = local_gram(x)
    got = lax.ppermute(send, "c", [(0, 1), (1, 0)])
    part = (keep + got).reshape(sharers, 1, -1)
    part = jnp.sum(lax.all_to_all(part, SUM_AXES, 0, 0, tiled=True), axis=0, keepdims=True)
    part = jnp.broadcast_to(part, (sharers, 1, part.shape[2]))
    mine = lax.all_to_all(part, SUM_AXES, 0, 0, tiled=True).reshape(SHARE, WIDE, WIDE)
    other = lax.ppermute(mine, "c", [(0, 1), (1, 0)])
    y, norms = chain(mine, other, x)
    out = lax.all_to_all(y.reshape(snapshots.shape), PAIR_AXES, 0, 0, tiled=True)
    return out, norms.reshape(WIDE)


def solution(mesh):
    axes = ("yl", "z", "c", "x", "yh")
    finer = jax.sharding.Mesh(mesh.devices.reshape(2, 8, 2, 4, 2), axes)
    rows, pairs = ("yl", "z", "c"), PAIR_AXES
    return jax.shard_map(
        body,
        mesh=finer,
        in_specs=(P(rows, pairs),),
        out_specs=(P(rows, pairs), P(pairs)),
        check_vma=False,
    )
```

```python
import jax
import jax.numpy as jnp
import numpy as np
from jax import lax
from jax.experimental import pallas as pl
from jax.experimental.pallas import tpu as pltpu
from jax.sharding import PartitionSpec as P

STEPS = 6
HALF = 64
WIDE = 2 * HALF
PAIRS = 8
BLOCKS = [(i, j) for i in range(PAIRS) for j in range(i, PAIRS)]
INDEX = {block: t for t, block in enumerate(BLOCKS)}
SHARE = len(BLOCKS) // 2

PAIR_AXES = ("x", "yh")
PLANE_AXES = ("yl", "x", "yh")
F32 = jnp.float32
BF16 = jnp.bfloat16
VMEM_LIMIT = 60 * 1024 * 1024

MOVED = {0: 0, 1: 2, 2 * PAIRS - 2: 2 * PAIRS - 1}
for place in range(1, PAIRS - 1):
    MOVED[2 * place] = 2 * (place + 1)
for place in range(1, PAIRS):
    MOVED[2 * place + 1] = 2 * (place - 1) + 1


def sources(block):
    return [next(t for t, u in MOVED.items() if u == b) for b in block]


def updates():
    lists = []
    needed = {(2 * k + a, 2 * k + b) for k in range(PAIRS) for a in range(2) for b in range(a, 2)}
    inside = set(needed)
    for _ in range(STEPS - 1):
        blocks = set()
        for block in needed:
            old = sorted(sources(block))
            blocks.add((old[0] // 2, old[1] // 2))
        lists.insert(0, sorted(blocks))
        needed = set(inside)
        for i, j in blocks:
            needed |= {tuple(sorted((2 * i + a, 2 * j + b))) for a in range(2) for b in range(2)}
    return lists


KMODE = True


def split(x):
    high = x.astype(BF16)
    low = (x - high.astype(F32)).astype(BF16)
    return high, low


def left(x, k=None):
    return jnp.concatenate(split(x), axis=1 if (KMODE if k is None else k) else 0)


def right(x, k=None):
    both = jnp.concatenate(split(x), axis=1)
    return jnp.concatenate([both, both], axis=0) if (KMODE if k is None else k) else both


def mul(a, b, k=None):
    y = jnp.dot(a, b, preferred_element_type=F32)
    if not (KMODE if k is None else k):
        m = y.shape[0] // 2
        y = y[:m] + y[m:]
    n = y.shape[1] // 2
    return y[:, :n] + y[:, n:]


def gram_kernel(x_ref, keep_ref, send_ref, lhs, rhs):
    core = lax.axis_index("c")
    for k in range(PAIRS):
        x = x_ref[k]
        rhs[k] = jnp.concatenate(split(x), axis=1)
        lhs[k] = jnp.concatenate(split(x.T), axis=0)

    def block(i, j):
        y = jnp.dot(lhs[i], rhs[j], preferred_element_type=F32)
        y = y[:WIDE] + y[WIDE:]
        return y[:, :WIDE] + y[:, WIDE:]

    for t in range(SHARE):
        first = block(*BLOCKS[t])
        second = block(*BLOCKS[t + SHARE])
        keep_ref[t] = jnp.where(core == 0, first, second)
        send_ref[t] = jnp.where(core == 0, second, first)


def chain_kernel(mine_ref, other_ref, x_ref, y_ref, norms_ref, gram, half, data, data_left, skew, inv, power, turn, turned, norms):
    core = lax.axis_index("c")
    position = lax.axis_index("x") * 2 + lax.axis_index("yh")
    row = lax.broadcasted_iota(jnp.int32, (WIDE, WIDE), 0)
    col = lax.broadcasted_iota(jnp.int32, (WIDE, WIDE), 1)
    eye = (row == col).astype(F32)
    for t in range(len(BLOCKS)):
        gram[t] = jnp.where(core == t // SHARE, mine_ref[t % SHARE], other_ref[t % SHARE])

    def rotations():
        radius = jnp.zeros((1, 1), F32)
        for k in range(PAIRS):
            g = gram[INDEX[k, k]]
            diag = g * eye
            total = jnp.sum(diag, axis=0, keepdims=True) + jnp.sum(diag, axis=1, keepdims=True)
            ratio = jnp.clip(0.5 * (g / total), -0.25, 0.25)
            s = jnp.where(col > row, ratio, jnp.where(col < row, -ratio, 0.0))
            skew[k] = s
            square = mul(left(s), right(s))
            bound = jnp.sqrt(0.5 * jnp.sum(square * square, axis=(0, 1), keepdims=True)) * 1.001
            scale = 2.0 / (2.0 + bound)
            power[k] = (1.0 - scale) * eye + scale * square
            inv[k] = scale * (eye + s)
            radius = jnp.maximum(radius, bound / (2.0 + bound))

        def multiply_on(rate):
            for k in range(PAIRS):
                p = inv[k]
                r = power[k]
                y = mul(jnp.concatenate([left(p, True), left(r, True)], axis=0), right(r, True), True)
                inv[k] = p + y[:WIDE]
                power[k] = y[WIDE:]
            return rate * rate

        lax.while_loop(lambda rate: rate > 2e-3, multiply_on, radius[0, 0])

        def correct(carry):
            rounds, _ = carry
            worst = jnp.zeros((1, 1), F32)
            for k in range(PAIRS):
                p = inv[k]
                e = eye - p + mul(left(skew[k]), right(p))
                inv[k] = p + mul(left(p), right(e))
                worst = jnp.maximum(worst, jnp.sum(e * e, axis=(0, 1), keepdims=True))
            return rounds + 1, worst[0, 0]

        lax.while_loop(lambda c: jnp.logical_and(c[1] > 3e-5, c[0] < 40), correct, (0, jnp.float32(1.0)))

        for k in range(PAIRS):
            j = 2.0 * inv[k] - eye
            turn[k] = right(j)
            turned[k] = left(j.T)

    def put(ref, lead, value, a, b, to_a, to_b):
        part = value[a * HALF : (a + 1) * HALF, :]
        if b != to_b:
            part = pltpu.roll(part, HALF, 1)
        ref[lead, pl.ds(to_a * HALF, HALF), pl.ds(to_b * HALF, HALF)] = part[:, to_b * HALF : (to_b + 1) * HALF]

    def rotate_gram(blocks):
        for i, j in blocks:
            half[INDEX[i, j]] = right(mul(left(gram[INDEX[i, j]]), turn[j]), False)
        for i, j in blocks:
            h = half[INDEX[i, j]]
            g = mul(turned[i], jnp.concatenate([h, h], axis=0) if KMODE else h)
            flipped = None
            for a in range(2):
                for b in range(2):
                    to_i, to_j = MOVED[2 * i + a], MOVED[2 * j + b]
                    if i == j and a != b and to_i > to_j:
                        continue
                    low, high = min(to_i, to_j), max(to_i, to_j)
                    target = INDEX[low // 2, high // 2]
                    within = low // 2 == high // 2 and low != high
                    if to_i <= to_j or within:
                        put(gram, target, g, a, b, to_i % 2, to_j % 2)
                    if to_i > to_j or within:
                        flipped = g.T if flipped is None else flipped
                        put(gram, target, flipped, b, a, to_j % 2, to_i % 2)

    def moved(k, top, bottom):
        sides = []
        for side in range(2):
            (source,) = sources([2 * k + side])
            value = data[source // 2]
            sides.append(value if source % 2 == side else pltpu.roll(value, HALF, 1))
        lane = lax.broadcasted_iota(jnp.int32, sides[0].shape, 1)
        return jnp.where(lane < HALF, sides[0], sides[1])

    def rotate_data(s):
        @pl.when(s == 0)
        def _():
            for k in range(PAIRS):
                data_left[k] = left(x_ref[k])

        @pl.when(s > 0)
        def _():
            for k in range(PAIRS):
                data_left[k] = left(moved(k, 0, 0))

        for k in range(PAIRS):
            data[k] = mul(data_left[k], turn[k])

    lists = updates()

    def step(s, carry):
        rotations()
        for first in range(STEPS - 1):
            if first and lists[first] == lists[first - 1]:
                continue
            steps = [t for t in range(STEPS - 1) if lists[t] == lists[first]]

            @pl.when(jnp.logical_and(s >= steps[0], s <= steps[-1]))
            def _():
                rotate_gram(lists[first])

        rotate_data(s)
        return carry

    lax.fori_loop(0, STEPS, step, 0)
    for k in range(PAIRS):
        y_ref[k] = moved(k, 0, 0)
    for k in range(PAIRS):
        j = 2.0 * inv[k] - eye
        h = mul(left(gram[INDEX[k, k]]), turn[k])
        n = jnp.sqrt(jnp.maximum(jnp.sum(j * h, axis=0, keepdims=True), 0.0))
        for b in range(2):
            to = MOVED[2 * k + b]
            part = n if b == to % 2 else pltpu.roll(n, HALF, 1)
            side = to % 2 * HALF
            norms[to // 2, :, pl.ds(side, HALF)] = part[:, side : side + HALF]
    norms_ref[...] = norms[position]


def local_gram(x):
    rows = x.shape[1]
    out = jax.ShapeDtypeStruct((SHARE, WIDE, WIDE), F32)
    return pl.pallas_call(
        gram_kernel,
        out_shape=(out, out),
        scratch_shapes=[
            pltpu.VMEM((PAIRS, 2 * WIDE, rows), BF16),
            pltpu.VMEM((PAIRS, rows, 2 * WIDE), BF16),
        ],
        compiler_params=pltpu.CompilerParams(vmem_limit_bytes=VMEM_LIMIT),
        name="gram",
    )(x)


def chain(mine, other, x):
    rows = x.shape[1]
    square = pltpu.VMEM((PAIRS, WIDE, WIDE), F32)
    return pl.pallas_call(
        chain_kernel,
        out_shape=(
            jax.ShapeDtypeStruct((PAIRS, rows, WIDE), F32),
            jax.ShapeDtypeStruct((1, WIDE), F32),
        ),
        scratch_shapes=[
            pltpu.VMEM((len(BLOCKS), WIDE, WIDE), F32),
            pltpu.VMEM((len(BLOCKS), WIDE, 2 * WIDE), BF16),
            pltpu.VMEM((PAIRS, rows, WIDE), F32),
            pltpu.VMEM((PAIRS, rows, 2 * WIDE) if KMODE else (PAIRS, 2 * rows, WIDE), BF16),
            square,
            square,
            square,
            pltpu.VMEM((PAIRS, 2 * WIDE, 2 * WIDE) if KMODE else (PAIRS, WIDE, 2 * WIDE), BF16),
            pltpu.VMEM((PAIRS, WIDE, 2 * WIDE) if KMODE else (PAIRS, 2 * WIDE, WIDE), BF16),
            pltpu.VMEM((PAIRS, 1, WIDE), F32),
        ],
        compiler_params=pltpu.CompilerParams(vmem_limit_bytes=VMEM_LIMIT),
        name="chain",
    )(mine, other, x)


def swapped(x, axis, by):
    return lax.ppermute(x, axis, [(i, i ^ by) for i in range(lax.axis_size(axis))])


def body(snapshots):
    rows = snapshots.shape[0] // PAIRS
    sharers = lax.axis_size(PLANE_AXES)
    x = lax.all_to_all(snapshots, PAIR_AXES, 0, 0, tiled=True).reshape(PAIRS, rows, WIDE)
    keep, send = local_gram(x)
    part = (keep + swapped(send, "c", 1)).reshape(sharers, -1, WIDE)
    part = jnp.sum(lax.all_to_all(part, PLANE_AXES, 0, 0, tiled=True), axis=0)
    for by in (1, 2, 7):
        part = part + swapped(part, "z", by)
    part = jnp.broadcast_to(part[None], (sharers,) + part.shape)
    mine = lax.all_to_all(part, PLANE_AXES, 0, 0, tiled=True).reshape(SHARE, WIDE, WIDE)
    other = swapped(mine, "c", 1)
    y, norms = chain(mine, other, x)
    out = lax.all_to_all(y.reshape(snapshots.shape), PAIR_AXES, 0, 0, tiled=True)
    return out, norms.reshape(WIDE)


def solution(mesh):
    axes = ("yl", "z", "c", "x", "yh")
    finer = jax.sharding.Mesh(mesh.devices.reshape(2, 8, 2, 4, 2), axes)
    rows, pairs = ("yl", "z", "c"), PAIR_AXES
    return jax.shard_map(
        body,
        mesh=finer,
        in_specs=(P(rows, pairs),),
        out_specs=(P(rows, pairs), P(pairs)),
        check_vma=False,
    )
```

```python
import jax
import jax.numpy as jnp
from jax import lax
from jax.experimental import pallas as pl
from jax.experimental.pallas import tpu as pltpu
from jax.sharding import PartitionSpec as P

STEPS = 6
HALF = 64
WIDE = 2 * HALF
PAIRS = 8
BLOCKS = [(i, j) for i in range(PAIRS) for j in range(i, PAIRS)]
INDEX = {block: t for t, block in enumerate(BLOCKS)}
SHARE = len(BLOCKS) // 2

PAIR_AXES = ("x", "yh")
PLANE_AXES = ("yl", "x", "yh")
F32 = jnp.float32
BF16 = jnp.bfloat16
MIB = 1024 * 1024
DOUBLINGS = 4

MOVED = {0: 0, 1: 2, 2 * PAIRS - 2: 2 * PAIRS - 1}
for place in range(1, PAIRS - 1):
    MOVED[2 * place] = 2 * (place + 1)
for place in range(1, PAIRS):
    MOVED[2 * place + 1] = 2 * (place - 1) + 1


def sources(block):
    return [next(t for t, u in MOVED.items() if u == b) for b in block]


def updates():
    lists = []
    needed = {(2 * k + a, 2 * k + b) for k in range(PAIRS) for a in range(2) for b in range(a, 2)}
    inside = set(needed)
    for _ in range(STEPS - 1):
        blocks = set()
        for block in needed:
            old = sorted(sources(block))
            blocks.add((old[0] // 2, old[1] // 2))
        lists.insert(0, sorted(blocks))
        needed = set(inside)
        for i, j in blocks:
            needed |= {tuple(sorted((2 * i + a, 2 * j + b))) for a in range(2) for b in range(2)}
    return lists


def split(x):
    high = x.astype(BF16)
    low = (x - high.astype(F32)).astype(BF16)
    return high, low


def beside(x):
    return jnp.concatenate(split(x), axis=1)


def twice(both):
    return jnp.concatenate([both, both], axis=0)


def mul(a, b):
    y = jnp.dot(a, b, preferred_element_type=F32)
    n = y.shape[1] // 2
    return y[:, :n] + y[:, n:]


def gram_kernel(x_ref, keep_ref, send_ref, lhs, rhs):
    core = lax.axis_index("c")
    for k in range(PAIRS):
        x = x_ref[k]
        rhs[k] = jnp.concatenate(split(x), axis=1)
        lhs[k] = jnp.concatenate(split(x.T), axis=0)

    def block(i, j):
        y = jnp.dot(lhs[i], rhs[j], preferred_element_type=F32)
        y = y[:WIDE] + y[WIDE:]
        return y[:, :WIDE] + y[:, WIDE:]

    for t in range(SHARE):
        first = block(*BLOCKS[t])
        second = block(*BLOCKS[t + SHARE])
        keep_ref[t] = jnp.where(core == 0, first, second)
        send_ref[t] = jnp.where(core == 0, second, first)


def chain_kernel(mine_ref, other_ref, x_ref, y_ref, norms_ref, gram, half, data, after, skew, inv, turn, turned, norms):
    core = lax.axis_index("c")
    position = lax.axis_index("x") * 2 + lax.axis_index("yh")
    row = lax.broadcasted_iota(jnp.int32, (WIDE, WIDE), 0)
    col = lax.broadcasted_iota(jnp.int32, (WIDE, WIDE), 1)
    eye = (row == col).astype(F32)
    for t in range(len(BLOCKS)):
        gram[t] = jnp.where(core == t // SHARE, mine_ref[t % SHARE], other_ref[t % SHARE])
    for k in range(PAIRS):
        data[k] = beside(x_ref[k])

    def correct(k):
        p = inv[k]
        e = eye - p + mul(beside(skew[k]), twice(beside(p)))
        inv[k] = p + jnp.dot(p.astype(BF16), e.astype(BF16), preferred_element_type=F32)
        return jnp.sum(e * e, axis=(0, 1), keepdims=True)

    def correct_all():
        worst = jnp.zeros((1, 1), F32)
        for k in range(PAIRS):
            worst = jnp.maximum(worst, correct(k))
        return worst[0, 0]

    def rotations():
        powers, rates = [], []
        for k in range(PAIRS):
            g = gram[INDEX[k, k]]
            diag = g * eye
            total = jnp.sum(diag, axis=0, keepdims=True) + jnp.sum(diag, axis=1, keepdims=True)
            ratio = jnp.clip(0.5 * (g / total), -0.25, 0.25)
            s = jnp.where(col > row, ratio, jnp.where(col < row, -ratio, 0.0))
            skew[k] = s
            both = beside(s)
            square = mul(both, twice(both))
            bound = jnp.sqrt(0.5 * jnp.sum(square * square, axis=(0, 1), keepdims=True)) * 1.001
            scale = 2.0 / (2.0 + bound)
            powers.append((1.0 - scale) * eye + scale * square)
            inv[k] = scale * (eye + s)
            rates.append(bound / (2.0 + bound))
        for time in range(DOUBLINGS):
            last = time == DOUBLINGS - 1
            for k in range(PAIRS):
                p = inv[k]
                both = beside(powers[k])
                stack = beside(p) if last else jnp.concatenate([beside(p), both], axis=0)
                y = mul(stack, twice(both))
                rate = rates[k] * rates[k] / (2.0 - rates[k] * rates[k])
                inv[k] = (1.0 + rate) * (p + y[:WIDE])
                if not last:
                    powers[k] = (1.0 + rate) * y[WIDE:] - rate * eye
                rates[k] = rate
        lax.while_loop(
            lambda c: jnp.logical_and(c[1] > 3e-5, c[0] < 40),
            lambda c: (c[0] + 1, correct_all()),
            (0, correct_all()),
        )
        for k in range(PAIRS):
            j = 2.0 * inv[k] - eye
            turn[k] = twice(beside(j))
            turned[k] = beside(j.T)

    def put(ref, lead, value, a, b, to_a, to_b):
        part = value[a * HALF : (a + 1) * HALF, :]
        if b != to_b:
            part = pltpu.roll(part, HALF, 1)
        ref[lead, pl.ds(to_a * HALF, HALF), pl.ds(to_b * HALF, HALF)] = part[:, to_b * HALF : (to_b + 1) * HALF]

    def rotate_gram(blocks):
        for i, j in blocks:
            half[INDEX[i, j]] = beside(mul(beside(gram[INDEX[i, j]]), turn[j]))
        for i, j in blocks:
            g = mul(turned[i], twice(half[INDEX[i, j]]))
            flipped = None
            for a in range(2):
                for b in range(2):
                    to_i, to_j = MOVED[2 * i + a], MOVED[2 * j + b]
                    if i == j and a != b and to_i > to_j:
                        continue
                    low, high = min(to_i, to_j), max(to_i, to_j)
                    target = INDEX[low // 2, high // 2]
                    within = low // 2 == high // 2 and low != high
                    if to_i <= to_j or within:
                        put(gram, target, g, a, b, to_i % 2, to_j % 2)
                    if to_i > to_j or within:
                        flipped = g.T if flipped is None else flipped
                        put(gram, target, flipped, b, a, to_j % 2, to_i % 2)

    def halves(k, value):
        for b in range(2):
            to = MOVED[2 * k + b]
            yield to // 2, to % 2 * HALF, value if b == to % 2 else pltpu.roll(value, HALF, 1)

    def rotate_data(now, later):
        for k in range(PAIRS):
            for to, side, part in halves(k, mul(now[k], turn[k])):
                high, low = split(part)
                later[to, :, pl.ds(side, HALF)] = high[:, side : side + HALF]
                later[to, :, pl.ds(WIDE + side, HALF)] = low[:, side : side + HALF]

    lists = updates() + [[]]

    def two_steps(trip, carry):
        for odd in range(2):
            rotations()
            for t in range(STEPS // 2):

                @pl.when(trip == t)
                def _():
                    rotate_gram(lists[2 * t + odd])

            if odd == 0:
                rotate_data(data, after)
            else:

                @pl.when(trip < STEPS // 2 - 1)
                def _():
                    rotate_data(after, data)

        return carry

    lax.fori_loop(0, STEPS // 2, two_steps, 0)
    for k in range(PAIRS):
        for to, side, part in halves(k, mul(after[k], turn[k])):
            y_ref[to, :, pl.ds(side, HALF)] = part[:, side : side + HALF]
    for k in range(PAIRS):
        j = 2.0 * inv[k] - eye
        h = mul(beside(gram[INDEX[k, k]]), turn[k])
        n = jnp.sqrt(jnp.maximum(jnp.sum(j * h, axis=0, keepdims=True), 0.0))
        for to, side, part in halves(k, n):
            norms[to, :, pl.ds(side, HALF)] = part[:, side : side + HALF]
    norms_ref[...] = norms[position]


def local_gram(x):
    rows = x.shape[1]
    out = jax.ShapeDtypeStruct((SHARE, WIDE, WIDE), F32)
    return pl.pallas_call(
        gram_kernel,
        out_shape=(out, out),
        scratch_shapes=[
            pltpu.VMEM((PAIRS, 2 * WIDE, rows), BF16),
            pltpu.VMEM((PAIRS, rows, 2 * WIDE), BF16),
        ],
        compiler_params=pltpu.CompilerParams(vmem_limit_bytes=16 * MIB),
        name="gram",
    )(x)


def chain(mine, other, x):
    rows = x.shape[1]
    square = pltpu.VMEM((PAIRS, WIDE, WIDE), F32)
    return pl.pallas_call(
        chain_kernel,
        out_shape=(
            jax.ShapeDtypeStruct((PAIRS, rows, WIDE), F32),
            jax.ShapeDtypeStruct((1, WIDE), F32),
        ),
        scratch_shapes=[
            pltpu.VMEM((len(BLOCKS), WIDE, WIDE), F32),
            pltpu.VMEM((len(BLOCKS), WIDE, 2 * WIDE), BF16),
            pltpu.VMEM((PAIRS, rows, 2 * WIDE), BF16),
            pltpu.VMEM((PAIRS, rows, 2 * WIDE), BF16),
            square,
            square,
            pltpu.VMEM((PAIRS, 2 * WIDE, 2 * WIDE), BF16),
            pltpu.VMEM((PAIRS, WIDE, 2 * WIDE), BF16),
            pltpu.VMEM((PAIRS, 1, WIDE), F32),
        ],
        compiler_params=pltpu.CompilerParams(vmem_limit_bytes=32 * MIB),
        name="chain",
    )(mine, other, x)


def swapped(x, axis, by):
    return lax.ppermute(x, axis, [(i, i ^ by) for i in range(lax.axis_size(axis))])


def body(snapshots):
    rows = snapshots.shape[0] // PAIRS
    sharers = lax.axis_size(PLANE_AXES)
    x = lax.all_to_all(snapshots, PAIR_AXES, 0, 0, tiled=True).reshape(PAIRS, rows, WIDE)
    keep, send = local_gram(x)
    part = (keep + swapped(send, "c", 1)).reshape(sharers, -1, WIDE)
    part = jnp.sum(lax.all_to_all(part, PLANE_AXES, 0, 0, tiled=True), axis=0)
    for by in (1, 2, 7):
        part = part + swapped(part, "z", by)
    part = jnp.broadcast_to(part[None], (sharers,) + part.shape)
    mine = lax.all_to_all(part, PLANE_AXES, 0, 0, tiled=True).reshape(SHARE, WIDE, WIDE)
    other = swapped(mine, "c", 1)
    y, norms = chain(mine, other, x)
    out = lax.all_to_all(y.reshape(snapshots.shape), PAIR_AXES, 0, 0, tiled=True)
    return out, norms.reshape(WIDE)


def solution(mesh):
    axes = ("yl", "z", "c", "x", "yh")
    finer = jax.sharding.Mesh(mesh.devices.reshape(2, 8, 2, 4, 2), axes)
    rows, pairs = ("yl", "z", "c"), PAIR_AXES
    return jax.shard_map(
        body,
        mesh=finer,
        in_specs=(P(rows, pairs),),
        out_specs=(P(rows, pairs), P(pairs)),
        check_vma=False,
    )
```

```python
import jax
import jax.numpy as jnp
from jax import lax
from jax.experimental import pallas as pl
from jax.experimental.pallas import tpu as pltpu
from jax.sharding import PartitionSpec as P

STEPS = 6
HALF = 64
WIDE = 2 * HALF
PAIRS = 8
BLOCKS = [(i, j) for i in range(PAIRS) for j in range(i, PAIRS)]
INDEX = {block: t for t, block in enumerate(BLOCKS)}
SHARE = len(BLOCKS) // 2

PAIR_AXES = ("x", "yh")
PLANE_AXES = ("yl", "x", "yh")
F32 = jnp.float32
BF16 = jnp.bfloat16
MIB = 1024 * 1024
DOUBLINGS = 4
GROUP = 4

MOVED = {0: 0, 1: 2, 2 * PAIRS - 2: 2 * PAIRS - 1}
for place in range(1, PAIRS - 1):
    MOVED[2 * place] = 2 * (place + 1)
for place in range(1, PAIRS):
    MOVED[2 * place + 1] = 2 * (place - 1) + 1


def sources(block):
    return [next(t for t, u in MOVED.items() if u == b) for b in block]


def updates():
    lists = []
    needed = {(2 * k + a, 2 * k + b) for k in range(PAIRS) for a in range(2) for b in range(a, 2)}
    inside = set(needed)
    for _ in range(STEPS - 1):
        blocks = set()
        for block in needed:
            old = sorted(sources(block))
            blocks.add((old[0] // 2, old[1] // 2))
        lists.insert(0, sorted(blocks))
        needed = set(inside)
        for i, j in blocks:
            needed |= {tuple(sorted((2 * i + a, 2 * j + b))) for a in range(2) for b in range(2)}
    return lists


def split(x):
    high = x.astype(BF16)
    low = (x - high.astype(F32)).astype(BF16)
    return high, low


def beside(x):
    return jnp.concatenate(split(x), axis=1)


def twice(both):
    return jnp.concatenate([both, both], axis=0)


def three(x):
    high, middle = split(x)
    low = (x - high.astype(F32) - middle.astype(F32)).astype(BF16)
    return jnp.concatenate([high, middle], axis=1), low


def mul(a, b):
    y = jnp.dot(a, b, preferred_element_type=F32)
    n = y.shape[1] // 2
    return y[:, :n] + y[:, n:]


def gram_kernel(x_ref, keep_ref, send_ref, rhs, lhs):
    core = lax.axis_index("c")
    for k in range(PAIRS):
        x = x_ref[k]
        rhs[k] = beside(x)
        lhs[k] = jnp.concatenate(split(x.T), axis=0)

    def block(i, j):
        y = jnp.dot(lhs[i], rhs[j], preferred_element_type=F32)
        y = y[:WIDE] + y[WIDE:]
        return y[:, :WIDE] + y[:, WIDE:]

    for t in range(SHARE):
        first = block(*BLOCKS[t])
        second = block(*BLOCKS[t + SHARE])
        keep_ref[t] = jnp.where(core == 0, first, second)
        send_ref[t] = jnp.where(core == 0, second, first)


def chain_kernel(mine_ref, other_ref, x_ref, y_ref, norms_ref, gram, half, rest, data, after, skew, inv, turn, turned, norms):
    core = lax.axis_index("c")
    position = lax.axis_index("x") * 2 + lax.axis_index("yh")
    row = lax.broadcasted_iota(jnp.int32, (WIDE, WIDE), 0)
    col = lax.broadcasted_iota(jnp.int32, (WIDE, WIDE), 1)
    eye = (row == col).astype(F32)
    for t in range(len(BLOCKS)):
        gram[t] = jnp.where(core == t // SHARE, mine_ref[t % SHARE], other_ref[t % SHARE])

    def correct(k):
        p = inv[k]
        e = eye - p + mul(beside(skew[k]), twice(beside(p)))
        inv[k] = p + jnp.dot(p.astype(BF16), e.astype(BF16), preferred_element_type=F32)
        return jnp.sum(e * e, axis=(0, 1), keepdims=True)

    def correct_all():
        worst = jnp.zeros((1, 1), F32)
        for k in range(PAIRS):
            worst = jnp.maximum(worst, correct(k))
        return worst[0, 0]

    def rotations():
        powers, rates = [], []
        for k in range(PAIRS):
            g = gram[INDEX[k, k]]
            diag = g * eye
            total = jnp.sum(diag, axis=0, keepdims=True) + jnp.sum(diag, axis=1, keepdims=True)
            ratio = jnp.clip(0.5 * (g / total), -0.25, 0.25)
            s = jnp.where(col > row, ratio, jnp.where(col < row, -ratio, 0.0))
            skew[k] = s
            both = beside(s)
            square = mul(both, twice(both))
            bound = jnp.sqrt(0.5 * jnp.sum(square * square, axis=(0, 1), keepdims=True)) * 1.001
            scale = 2.0 / (2.0 + bound)
            powers.append((1.0 - scale) * eye + scale * square)
            inv[k] = scale * (eye + s)
            rates.append(bound / (2.0 + bound))
        for time in range(DOUBLINGS):
            last = time == DOUBLINGS - 1
            for k in range(PAIRS):
                p = inv[k]
                both = beside(powers[k])
                stack = beside(p) if last else jnp.concatenate([beside(p), both], axis=0)
                y = mul(stack, twice(both))
                rate = rates[k] * rates[k] / (2.0 - rates[k] * rates[k])
                inv[k] = (1.0 + rate) * (p + y[:WIDE])
                if not last:
                    powers[k] = (1.0 + rate) * y[WIDE:] - rate * eye
                rates[k] = rate
        lax.while_loop(
            lambda c: jnp.logical_and(c[1] > 3e-5, c[0] < 40),
            lambda c: (c[0] + 1, correct_all()),
            (0, correct_all()),
        )
        for k in range(PAIRS):
            j = 2.0 * inv[k] - eye
            turn[k] = twice(beside(j))
            turned[k] = beside(j.T)

    def put(ref, lead, value, a, b, to_a, to_b):
        part = value[a * HALF : (a + 1) * HALF, :]
        if b != to_b:
            part = pltpu.roll(part, HALF, 1)
        ref[lead, pl.ds(to_a * HALF, HALF), pl.ds(to_b * HALF, HALF)] = part[:, to_b * HALF : (to_b + 1) * HALF]

    def rotate_gram(blocks):
        for j in range(PAIRS):
            column = [INDEX[block] for block in blocks if block[1] == j]
            for start in range(0, len(column), GROUP):
                group = column[start : start + GROUP]
                parts = [three(gram[t]) for t in group]
                h = mul(jnp.concatenate([both for both, _ in parts], axis=0), turn[j])
                low = jnp.concatenate([low for _, low in parts], axis=0)
                h = h + jnp.dot(low, turn[j, :WIDE, :WIDE], preferred_element_type=F32)
                for place, t in enumerate(group):
                    half[t], rest[t] = three(h[place * WIDE : (place + 1) * WIDE])
        for i, j in blocks:
            t = INDEX[i, j]
            g = mul(turned[i], twice(half[t])) + jnp.dot(turned[i, :, :WIDE], rest[t], preferred_element_type=F32)
            flipped = None
            for a in range(2):
                for b in range(2):
                    to_i, to_j = MOVED[2 * i + a], MOVED[2 * j + b]
                    if i == j and a != b and to_i > to_j:
                        continue
                    low, high = min(to_i, to_j), max(to_i, to_j)
                    target = INDEX[low // 2, high // 2]
                    within = low // 2 == high // 2 and low != high
                    if to_i <= to_j or within:
                        put(gram, target, g, a, b, to_i % 2, to_j % 2)
                    if to_i > to_j or within:
                        flipped = g.T if flipped is None else flipped
                        put(gram, target, flipped, b, a, to_j % 2, to_i % 2)

    def halves(k, value):
        for b in range(2):
            to = MOVED[2 * k + b]
            yield to // 2, to % 2 * HALF, value if b == to % 2 else pltpu.roll(value, HALF, 1)

    def rotate_data(now, later):
        for k in range(PAIRS):
            for to, side, part in halves(k, mul(now[k], turn[k])):
                high, low = split(part)
                later[to, :, pl.ds(side, HALF)] = high[:, side : side + HALF]
                later[to, :, pl.ds(WIDE + side, HALF)] = low[:, side : side + HALF]

    lists = updates() + [[]]

    def two_steps(trip, carry):
        for odd in range(2):
            rotations()
            for t in range(STEPS // 2):

                @pl.when(trip == t)
                def _():
                    rotate_gram(lists[2 * t + odd])

            if odd == 0:

                @pl.when(trip == 0)
                def _():
                    rotate_data(x_ref, after)

                @pl.when(trip > 0)
                def _():
                    rotate_data(data, after)

            else:

                @pl.when(trip < STEPS // 2 - 1)
                def _():
                    rotate_data(after, data)

        return carry

    lax.fori_loop(0, STEPS // 2, two_steps, 0)
    for k in range(PAIRS):
        for to, side, part in halves(k, mul(after[k], turn[k])):
            y_ref[to, :, pl.ds(side, HALF)] = part[:, side : side + HALF]
    for k in range(PAIRS):
        j = 2.0 * inv[k] - eye
        h = mul(beside(gram[INDEX[k, k]]), turn[k])
        n = jnp.sqrt(jnp.maximum(jnp.sum(j * h, axis=0, keepdims=True), 0.0))
        for to, side, part in halves(k, n):
            norms[to, :, pl.ds(side, HALF)] = part[:, side : side + HALF]
    norms_ref[...] = norms[position]


def local_gram(x):
    rows = x.shape[1]
    out = jax.ShapeDtypeStruct((SHARE, WIDE, WIDE), F32)
    return pl.pallas_call(
        gram_kernel,
        out_shape=(out, out, jax.ShapeDtypeStruct((PAIRS, rows, 2 * WIDE), BF16)),
        scratch_shapes=[
            pltpu.VMEM((PAIRS, 2 * WIDE, rows), BF16),
        ],
        compiler_params=pltpu.CompilerParams(vmem_limit_bytes=16 * MIB),
        name="gram",
    )(x)


def chain(mine, other, x):
    rows = x.shape[1]
    square = pltpu.VMEM((PAIRS, WIDE, WIDE), F32)
    return pl.pallas_call(
        chain_kernel,
        out_shape=(
            jax.ShapeDtypeStruct((PAIRS, rows, WIDE), F32),
            jax.ShapeDtypeStruct((1, WIDE), F32),
        ),
        scratch_shapes=[
            pltpu.VMEM((len(BLOCKS), WIDE, WIDE), F32),
            pltpu.VMEM((len(BLOCKS), WIDE, 2 * WIDE), BF16),
            pltpu.VMEM((len(BLOCKS), WIDE, WIDE), BF16),
            pltpu.VMEM((PAIRS, rows, 2 * WIDE), BF16),
            pltpu.VMEM((PAIRS, rows, 2 * WIDE), BF16),
            square,
            square,
            pltpu.VMEM((PAIRS, 2 * WIDE, 2 * WIDE), BF16),
            pltpu.VMEM((PAIRS, WIDE, 2 * WIDE), BF16),
            pltpu.VMEM((PAIRS, 1, WIDE), F32),
        ],
        compiler_params=pltpu.CompilerParams(vmem_limit_bytes=32 * MIB),
        name="chain",
    )(mine, other, x)


def swapped(x, axis, by):
    return lax.ppermute(x, axis, [(i, i ^ by) for i in range(lax.axis_size(axis))])


def body(snapshots):
    rows = snapshots.shape[0] // PAIRS
    sharers = lax.axis_size(PLANE_AXES)
    x = lax.all_to_all(snapshots, PAIR_AXES, 0, 0, tiled=True).reshape(PAIRS, rows, WIDE)
    keep, send, x = local_gram(x)
    part = (keep + swapped(send, "c", 1)).reshape(sharers, -1, WIDE)
    part = jnp.sum(lax.all_to_all(part, PLANE_AXES, 0, 0, tiled=True), axis=0)
    for by in (1, 2, 7):
        part = part + swapped(part, "z", by)
    part = jnp.broadcast_to(part[None], (sharers,) + part.shape)
    mine = lax.all_to_all(part, PLANE_AXES, 0, 0, tiled=True).reshape(SHARE, WIDE, WIDE)
    other = swapped(mine, "c", 1)
    y, norms = chain(mine, other, x)
    out = lax.all_to_all(y.reshape(snapshots.shape), PAIR_AXES, 0, 0, tiled=True)
    return out, norms.reshape(WIDE)


def solution(mesh):
    axes = ("yl", "z", "c", "x", "yh")
    finer = jax.sharding.Mesh(mesh.devices.reshape(2, 8, 2, 4, 2), axes)
    rows, pairs = ("yl", "z", "c"), PAIR_AXES
    return jax.shard_map(
        body,
        mesh=finer,
        in_specs=(P(rows, pairs),),
        out_specs=(P(rows, pairs), P(pairs)),
        check_vma=False,
    )
```

```python
import jax
import jax.numpy as jnp
from jax import lax
from jax.experimental import pallas as pl
from jax.experimental.pallas import tpu as pltpu
from jax.sharding import PartitionSpec as P

STEPS = 6
HALF = 64
WIDE = 2 * HALF
PAIRS = 8
BLOCKS = [(i, j) for i in range(PAIRS) for j in range(i, PAIRS)]
INDEX = {block: t for t, block in enumerate(BLOCKS)}
SHARE = len(BLOCKS) // 2

PAIR_AXES = ("x", "yh")
PLANE_AXES = ("yl", "x", "yh")
F32 = jnp.float32
BF16 = jnp.bfloat16
MIB = 1024 * 1024
DOUBLINGS = 4
GROUP = 8

MOVED = {0: 0, 1: 2, 2 * PAIRS - 2: 2 * PAIRS - 1}
for place in range(1, PAIRS - 1):
    MOVED[2 * place] = 2 * (place + 1)
for place in range(1, PAIRS):
    MOVED[2 * place + 1] = 2 * (place - 1) + 1


def sources(block):
    return [next(t for t, u in MOVED.items() if u == b) for b in block]


def updates():
    lists = []
    needed = {(2 * k + a, 2 * k + b) for k in range(PAIRS) for a in range(2) for b in range(a, 2)}
    inside = set(needed)
    for _ in range(STEPS - 1):
        blocks = set()
        for block in needed:
            old = sorted(sources(block))
            blocks.add((old[0] // 2, old[1] // 2))
        lists.insert(0, sorted(blocks))
        needed = set(inside)
        for i, j in blocks:
            needed |= {tuple(sorted((2 * i + a, 2 * j + b))) for a in range(2) for b in range(2)}
    return lists


def split(x):
    high = x.astype(BF16)
    low = (x - high.astype(F32)).astype(BF16)
    return high, low


def beside(x):
    return jnp.concatenate(split(x), axis=1)


def twice(both):
    return jnp.concatenate([both, both], axis=0)


def three(x):
    high, middle = split(x)
    low = (x - high.astype(F32) - middle.astype(F32)).astype(BF16)
    return jnp.concatenate([high, middle], axis=1), low


def mul(a, b):
    y = jnp.dot(a, b, preferred_element_type=F32)
    n = y.shape[1] // 2
    return y[:, :n] + y[:, n:]


def gram_kernel(x_ref, keep_ref, send_ref, rhs, lhs):
    core = lax.axis_index("c")
    for k in range(PAIRS):
        x = x_ref[k]
        rhs[k] = beside(x)
        lhs[k] = jnp.concatenate(split(x.T), axis=0)

    def block(i, j):
        y = jnp.dot(lhs[i], rhs[j], preferred_element_type=F32)
        y = y[:WIDE] + y[WIDE:]
        return y[:, :WIDE] + y[:, WIDE:]

    for t in range(SHARE):
        first = block(*BLOCKS[t])
        second = block(*BLOCKS[t + SHARE])
        keep_ref[t] = jnp.where(core == 0, first, second)
        send_ref[t] = jnp.where(core == 0, second, first)


def chain_kernel(mine_ref, other_ref, x_ref, y_ref, norms_ref, gram, half, rest, data, after, skew, inv, turn, turned, norms):
    core = lax.axis_index("c")
    position = lax.axis_index("x") * 2 + lax.axis_index("yh")
    row = lax.broadcasted_iota(jnp.int32, (WIDE, WIDE), 0)
    col = lax.broadcasted_iota(jnp.int32, (WIDE, WIDE), 1)
    eye = (row == col).astype(F32)
    for t in range(len(BLOCKS)):
        gram[t] = jnp.where(core == t // SHARE, mine_ref[t % SHARE], other_ref[t % SHARE])

    def correct(k):
        p = inv[k]
        e = eye - p + mul(beside(skew[k]), twice(beside(p)))
        inv[k] = p + jnp.dot(p.astype(BF16), e.astype(BF16), preferred_element_type=F32)
        return jnp.sum(e * e, axis=(0, 1), keepdims=True)

    def correct_all():
        worst = jnp.zeros((1, 1), F32)
        for k in range(PAIRS):
            worst = jnp.maximum(worst, correct(k))
        return worst[0, 0]

    def rotations():
        powers, rates = [], []
        for k in range(PAIRS):
            g = gram[INDEX[k, k]]
            diag = g * eye
            total = jnp.sum(diag, axis=0, keepdims=True) + jnp.sum(diag, axis=1, keepdims=True)
            ratio = jnp.clip(0.5 * (g / total), -0.25, 0.25)
            s = jnp.where(col > row, ratio, jnp.where(col < row, -ratio, 0.0))
            skew[k] = s
            both = beside(s)
            square = mul(both, twice(both))
            bound = jnp.sqrt(0.5 * jnp.sum(square * square, axis=(0, 1), keepdims=True)) * 1.001
            scale = 2.0 / (2.0 + bound)
            powers.append((1.0 - scale) * eye + scale * square)
            inv[k] = scale * (eye + s)
            rates.append(bound / (2.0 + bound))
        for time in range(DOUBLINGS):
            last = time == DOUBLINGS - 1
            for k in range(PAIRS):
                p = inv[k]
                both = beside(powers[k])
                stack = beside(p) if last else jnp.concatenate([beside(p), both], axis=0)
                y = mul(stack, twice(both))
                rate = rates[k] * rates[k] / (2.0 - rates[k] * rates[k])
                inv[k] = (1.0 + rate) * (p + y[:WIDE])
                if not last:
                    powers[k] = (1.0 + rate) * y[WIDE:] - rate * eye
                rates[k] = rate
        lax.while_loop(
            lambda c: jnp.logical_and(c[1] > 3e-5, c[0] < 40),
            lambda c: (c[0] + 1, correct_all()),
            (0, correct_all()),
        )
        for k in range(PAIRS):
            j = 2.0 * inv[k] - eye
            turn[k] = twice(beside(j))
            turned[k] = beside(j.T)

    def put(ref, lead, value, a, b, to_a, to_b):
        part = value[a * HALF : (a + 1) * HALF, :]
        if b != to_b:
            part = pltpu.roll(part, HALF, 1)
        ref[lead, pl.ds(to_a * HALF, HALF), pl.ds(to_b * HALF, HALF)] = part[:, to_b * HALF : (to_b + 1) * HALF]

    def rotate_gram(blocks):
        for j in range(PAIRS):
            column = [INDEX[block] for block in blocks if block[1] == j]
            for start in range(0, len(column), GROUP):
                group = column[start : start + GROUP]
                parts = [three(gram[t]) for t in group]
                h = mul(jnp.concatenate([both for both, _ in parts], axis=0), turn[j])
                low = jnp.concatenate([low for _, low in parts], axis=0)
                h = h + jnp.dot(low, turn[j, :WIDE, :WIDE], preferred_element_type=F32)
                for place, t in enumerate(group):
                    half[t], rest[t] = three(h[place * WIDE : (place + 1) * WIDE])
        for i, j in blocks:
            t = INDEX[i, j]
            g = mul(turned[i], twice(half[t])) + jnp.dot(turned[i, :, :WIDE], rest[t], preferred_element_type=F32)
            flipped = None
            for a in range(2):
                for b in range(2):
                    to_i, to_j = MOVED[2 * i + a], MOVED[2 * j + b]
                    if i == j and a != b and to_i > to_j:
                        continue
                    low, high = min(to_i, to_j), max(to_i, to_j)
                    target = INDEX[low // 2, high // 2]
                    within = low // 2 == high // 2 and low != high
                    if to_i <= to_j or within:
                        put(gram, target, g, a, b, to_i % 2, to_j % 2)
                    if to_i > to_j or within:
                        flipped = g.T if flipped is None else flipped
                        put(gram, target, flipped, b, a, to_j % 2, to_i % 2)

    def halves(k, value):
        for b in range(2):
            to = MOVED[2 * k + b]
            yield to // 2, to % 2 * HALF, value if b == to % 2 else pltpu.roll(value, HALF, 1)

    def rotate_data(now, later):
        for k in range(PAIRS):
            for to, side, part in halves(k, mul(now[k], turn[k])):
                high, low = split(part)
                later[to, :, pl.ds(side, HALF)] = high[:, side : side + HALF]
                later[to, :, pl.ds(WIDE + side, HALF)] = low[:, side : side + HALF]

    lists = updates() + [[]]

    def two_steps(trip, carry):
        for odd in range(2):
            rotations()
            for t in range(STEPS // 2):

                @pl.when(trip == t)
                def _():
                    now = after if odd else data if t else x_ref
                    if 2 * t + odd < STEPS - 1:
                        rotate_data(now, data if odd else after)
                    rotate_gram(lists[2 * t + odd])

        return carry

    lax.fori_loop(0, STEPS // 2, two_steps, 0)
    for k in range(PAIRS):
        for to, side, part in halves(k, mul(after[k], turn[k])):
            y_ref[to, :, pl.ds(side, HALF)] = part[:, side : side + HALF]
    for k in range(PAIRS):
        j = 2.0 * inv[k] - eye
        h = mul(beside(gram[INDEX[k, k]]), turn[k])
        n = jnp.sqrt(jnp.maximum(jnp.sum(j * h, axis=0, keepdims=True), 0.0))
        for to, side, part in halves(k, n):
            norms[to, :, pl.ds(side, HALF)] = part[:, side : side + HALF]
    norms_ref[...] = norms[position]


def local_gram(x):
    rows = x.shape[1]
    out = jax.ShapeDtypeStruct((SHARE, WIDE, WIDE), F32)
    return pl.pallas_call(
        gram_kernel,
        out_shape=(out, out, jax.ShapeDtypeStruct((PAIRS, rows, 2 * WIDE), BF16)),
        scratch_shapes=[
            pltpu.VMEM((PAIRS, 2 * WIDE, rows), BF16),
        ],
        compiler_params=pltpu.CompilerParams(vmem_limit_bytes=16 * MIB),
        name="gram",
    )(x)


def chain(mine, other, x):
    rows = x.shape[1]
    square = pltpu.VMEM((PAIRS, WIDE, WIDE), F32)
    return pl.pallas_call(
        chain_kernel,
        out_shape=(
            jax.ShapeDtypeStruct((PAIRS, rows, WIDE), F32),
            jax.ShapeDtypeStruct((1, WIDE), F32),
        ),
        scratch_shapes=[
            pltpu.VMEM((len(BLOCKS), WIDE, WIDE), F32),
            pltpu.VMEM((len(BLOCKS), WIDE, 2 * WIDE), BF16),
            pltpu.VMEM((len(BLOCKS), WIDE, WIDE), BF16),
            pltpu.VMEM((PAIRS, rows, 2 * WIDE), BF16),
            pltpu.VMEM((PAIRS, rows, 2 * WIDE), BF16),
            square,
            square,
            pltpu.VMEM((PAIRS, 2 * WIDE, 2 * WIDE), BF16),
            pltpu.VMEM((PAIRS, WIDE, 2 * WIDE), BF16),
            pltpu.VMEM((PAIRS, 1, WIDE), F32),
        ],
        compiler_params=pltpu.CompilerParams(vmem_limit_bytes=32 * MIB),
        name="chain",
    )(mine, other, x)


def swapped(x, axis, by):
    return lax.ppermute(x, axis, [(i, i ^ by) for i in range(lax.axis_size(axis))])


def body(snapshots):
    rows = snapshots.shape[0] // PAIRS
    sharers = lax.axis_size(PLANE_AXES)
    x = lax.all_to_all(snapshots, PAIR_AXES, 0, 0, tiled=True).reshape(PAIRS, rows, WIDE)
    keep, send, x = local_gram(x)
    part = (keep + swapped(send, "c", 1)).reshape(sharers, -1, WIDE)
    part = jnp.sum(lax.all_to_all(part, PLANE_AXES, 0, 0, tiled=True), axis=0)
    near, far, across = (swapped(part, "z", by) for by in (1, 2, 3))
    part = (part + near) + (far + across)
    part = part + swapped(part, "z", 7)
    part = jnp.broadcast_to(part[None], (sharers,) + part.shape)
    mine = lax.all_to_all(part, PLANE_AXES, 0, 0, tiled=True).reshape(SHARE, WIDE, WIDE)
    other = swapped(mine, "c", 1)
    y, norms = chain(mine, other, x)
    out = lax.all_to_all(y.reshape(snapshots.shape), PAIR_AXES, 0, 0, tiled=True)
    return out, norms.reshape(WIDE)


def solution(mesh):
    axes = ("yl", "z", "c", "x", "yh")
    finer = jax.sharding.Mesh(mesh.devices.reshape(2, 8, 2, 4, 2), axes)
    rows, pairs = ("yl", "z", "c"), PAIR_AXES
    return jax.shard_map(
        body,
        mesh=finer,
        in_specs=(P(rows, pairs),),
        out_specs=(P(rows, pairs), P(pairs)),
        check_vma=False,
    )
```

```python
import jax
import jax.numpy as jnp
from jax import lax
from jax.experimental import pallas as pl
from jax.experimental.pallas import tpu as pltpu
from jax.sharding import PartitionSpec as P

STEPS = 6
HALF = 64
WIDE = 2 * HALF
PAIRS = 8
BLOCKS = [(i, j) for i in range(PAIRS) for j in range(i, PAIRS)]
INDEX = {block: t for t, block in enumerate(BLOCKS)}
SHARE = len(BLOCKS) // 2

PAIR_AXES = ("x", "yh")
PLANE_AXES = ("yl", "x", "yh")
F32 = jnp.float32
BF16 = jnp.bfloat16
MIB = 1024 * 1024
DOUBLINGS = 4
GROUP = 8

MOVED = {0: 0, 1: 2, 2 * PAIRS - 2: 2 * PAIRS - 1}
for place in range(1, PAIRS - 1):
    MOVED[2 * place] = 2 * (place + 1)
for place in range(1, PAIRS):
    MOVED[2 * place + 1] = 2 * (place - 1) + 1


def sources(block):
    return [next(t for t, u in MOVED.items() if u == b) for b in block]


def updates():
    lists = []
    needed = {(2 * k + a, 2 * k + b) for k in range(PAIRS) for a in range(2) for b in range(a, 2)}
    inside = set(needed)
    for _ in range(STEPS - 1):
        blocks = set()
        for block in needed:
            old = sorted(sources(block))
            blocks.add((old[0] // 2, old[1] // 2))
        lists.insert(0, sorted(blocks))
        needed = set(inside)
        for i, j in blocks:
            needed |= {tuple(sorted((2 * i + a, 2 * j + b))) for a in range(2) for b in range(2)}
    return lists


def split(x):
    high = x.astype(BF16)
    low = (x - high.astype(F32)).astype(BF16)
    return high, low


def beside(x):
    return jnp.concatenate(split(x), axis=1)


def twice(both):
    return jnp.concatenate([both, both], axis=0)


def three(x):
    high, middle = split(x)
    low = (x - high.astype(F32) - middle.astype(F32)).astype(BF16)
    return jnp.concatenate([high, middle], axis=1), low


def mul(a, b):
    y = jnp.dot(a, b, preferred_element_type=F32)
    n = y.shape[1] // 2
    return y[:, :n] + y[:, n:]


def gram_kernel(x_ref, keep_ref, send_ref, rhs, lhs):
    core = lax.axis_index("c")
    for k in range(PAIRS):
        x = x_ref[k]
        rhs[k] = beside(x)
        lhs[k] = jnp.concatenate(split(x.T), axis=0)

    def block(i, j):
        y = jnp.dot(lhs[i], rhs[j], preferred_element_type=F32)
        y = y[:WIDE] + y[WIDE:]
        return y[:, :WIDE] + y[:, WIDE:]

    for t in range(SHARE):
        first = block(*BLOCKS[t])
        second = block(*BLOCKS[t + SHARE])
        keep_ref[t] = jnp.where(core == 0, first, second)
        send_ref[t] = jnp.where(core == 0, second, first)


def chain_kernel(mine_ref, other_ref, x_ref, y_ref, norms_ref, gram, half, rest, data, after, skew, inv, turn, turned, norms):
    core = lax.axis_index("c")
    position = lax.axis_index("x") * 2 + lax.axis_index("yh")
    row = lax.broadcasted_iota(jnp.int32, (WIDE, WIDE), 0)
    col = lax.broadcasted_iota(jnp.int32, (WIDE, WIDE), 1)
    eye = (row == col).astype(F32)
    for t in range(len(BLOCKS)):
        gram[t] = jnp.where(core == t // SHARE, mine_ref[t % SHARE], other_ref[t % SHARE])

    def correct(k):
        p = inv[k]
        e = eye - p + mul(beside(skew[k]), twice(beside(p)))
        inv[k] = p + jnp.dot(p.astype(BF16), e.astype(BF16), preferred_element_type=F32)
        return jnp.sum(e * e, axis=(0, 1), keepdims=True)

    def correct_all():
        worst = jnp.zeros((1, 1), F32)
        for k in range(PAIRS):
            worst = jnp.maximum(worst, correct(k))
        return worst[0, 0]

    def rotations():
        powers, rates = [], []
        for k in range(PAIRS):
            g = gram[INDEX[k, k]]
            diag = g * eye
            total = jnp.sum(diag, axis=0, keepdims=True) + jnp.sum(diag, axis=1, keepdims=True)
            ratio = jnp.clip(0.5 * (g / total), -0.25, 0.25)
            s = jnp.where(col > row, ratio, jnp.where(col < row, -ratio, 0.0))
            skew[k] = s
            both = beside(s)
            square = mul(both, twice(both))
            bound = jnp.sqrt(0.5 * jnp.sum(square * square, axis=(0, 1), keepdims=True)) * 1.001
            scale = 2.0 / (2.0 + bound)
            powers.append((1.0 - scale) * eye + scale * square)
            inv[k] = scale * (eye + s)
            rates.append(bound / (2.0 + bound))
        for time in range(DOUBLINGS):
            last = time == DOUBLINGS - 1
            for k in range(PAIRS):
                p = inv[k]
                both = beside(powers[k])
                stack = beside(p) if last else jnp.concatenate([beside(p), both], axis=0)
                y = mul(stack, twice(both))
                rate = rates[k] * rates[k] / (2.0 - rates[k] * rates[k])
                inv[k] = (1.0 + rate) * (p + y[:WIDE])
                if not last:
                    powers[k] = (1.0 + rate) * y[WIDE:] - rate * eye
                rates[k] = rate
        lax.while_loop(
            lambda c: jnp.logical_and(c[1] > 3e-5, c[0] < 40),
            lambda c: (c[0] + 1, correct_all()),
            (0, correct_all()),
        )
        for k in range(PAIRS):
            j = 2.0 * inv[k] - eye
            turn[k] = twice(beside(j))
            turned[k] = beside(j.T)

    def put(ref, lead, value, a, b, to_a, to_b):
        part = value[a * HALF : (a + 1) * HALF, :]
        if b != to_b:
            part = pltpu.roll(part, HALF, 1)
        ref[lead, pl.ds(to_a * HALF, HALF), pl.ds(to_b * HALF, HALF)] = part[:, to_b * HALF : (to_b + 1) * HALF]

    def rotate_gram(blocks):
        for j in range(PAIRS):
            column = [INDEX[block] for block in blocks if block[1] == j]
            for start in range(0, len(column), GROUP):
                group = column[start : start + GROUP]
                parts = [three(gram[t]) for t in group]
                h = mul(jnp.concatenate([both for both, _ in parts], axis=0), turn[j])
                low = jnp.concatenate([low for _, low in parts], axis=0)
                h = h + jnp.dot(low, turn[j, :WIDE, :WIDE], preferred_element_type=F32)
                for place, t in enumerate(group):
                    half[t], rest[t] = three(h[place * WIDE : (place + 1) * WIDE])
        for i, j in blocks:
            t = INDEX[i, j]
            g = mul(turned[i], twice(half[t])) + jnp.dot(turned[i, :, :WIDE], rest[t], preferred_element_type=F32)
            flipped = None
            for a in range(2):
                for b in range(2):
                    to_i, to_j = MOVED[2 * i + a], MOVED[2 * j + b]
                    if i == j and a != b and to_i > to_j:
                        continue
                    low, high = min(to_i, to_j), max(to_i, to_j)
                    target = INDEX[low // 2, high // 2]
                    within = low // 2 == high // 2 and low != high
                    if to_i <= to_j or within:
                        put(gram, target, g, a, b, to_i % 2, to_j % 2)
                    if to_i > to_j or within:
                        flipped = g.T if flipped is None else flipped
                        put(gram, target, flipped, b, a, to_j % 2, to_i % 2)

    def halves(k, value):
        for b in range(2):
            to = MOVED[2 * k + b]
            yield to // 2, to % 2 * HALF, value if b == to % 2 else pltpu.roll(value, HALF, 1)

    def rotate_data(now, later):
        for k in range(PAIRS):
            for to, side, part in halves(k, mul(now[k], turn[k])):
                high, low = split(part)
                later[to, :, pl.ds(side, HALF)] = high[:, side : side + HALF]
                later[to, :, pl.ds(WIDE + side, HALF)] = low[:, side : side + HALF]

    lists = updates() + [[]]

    def two_steps(trip, carry):
        for odd in range(2):
            rotations()
            for t in range(STEPS // 2):

                @pl.when(trip == t)
                def _():
                    now = after if odd else data if t else x_ref
                    if 2 * t + odd < STEPS - 1:
                        rotate_data(now, data if odd else after)
                    rotate_gram(lists[2 * t + odd])

        return carry

    lax.fori_loop(0, STEPS // 2, two_steps, 0)
    for k in range(PAIRS):
        for to, side, part in halves(k, mul(after[k], turn[k])):
            y_ref[to, :, pl.ds(side, HALF)] = part[:, side : side + HALF]
    for k in range(PAIRS):
        j = 2.0 * inv[k] - eye
        h = mul(beside(gram[INDEX[k, k]]), turn[k])
        n = jnp.sqrt(jnp.maximum(jnp.sum(j * h, axis=0, keepdims=True), 0.0))
        for to, side, part in halves(k, n):
            norms[to, :, pl.ds(side, HALF)] = part[:, side : side + HALF]
    norms_ref[...] = norms[position]


def local_gram(x):
    rows = x.shape[1]
    out = jax.ShapeDtypeStruct((SHARE, WIDE, WIDE), F32)
    return pl.pallas_call(
        gram_kernel,
        out_shape=(out, out, jax.ShapeDtypeStruct((PAIRS, rows, 2 * WIDE), BF16)),
        scratch_shapes=[
            pltpu.VMEM((PAIRS, 2 * WIDE, rows), BF16),
        ],
        compiler_params=pltpu.CompilerParams(vmem_limit_bytes=16 * MIB),
        name="gram",
    )(x)


def chain(mine, other, x):
    rows = x.shape[1]
    square = pltpu.VMEM((PAIRS, WIDE, WIDE), F32)
    return pl.pallas_call(
        chain_kernel,
        out_shape=(
            jax.ShapeDtypeStruct((PAIRS, rows, WIDE), F32),
            jax.ShapeDtypeStruct((1, WIDE), F32),
        ),
        scratch_shapes=[
            pltpu.VMEM((len(BLOCKS), WIDE, WIDE), F32),
            pltpu.VMEM((len(BLOCKS), WIDE, 2 * WIDE), BF16),
            pltpu.VMEM((len(BLOCKS), WIDE, WIDE), BF16),
            pltpu.VMEM((PAIRS, rows, 2 * WIDE), BF16),
            pltpu.VMEM((PAIRS, rows, 2 * WIDE), BF16),
            square,
            square,
            pltpu.VMEM((PAIRS, 2 * WIDE, 2 * WIDE), BF16),
            pltpu.VMEM((PAIRS, WIDE, 2 * WIDE), BF16),
            pltpu.VMEM((PAIRS, 1, WIDE), F32),
        ],
        compiler_params=pltpu.CompilerParams(vmem_limit_bytes=32 * MIB),
        name="chain",
    )(mine, other, x)


def swapped(x, axis, by):
    return lax.ppermute(x, axis, [(i, i ^ by) for i in range(lax.axis_size(axis))])


def body(snapshots):
    rows = snapshots.shape[0] // PAIRS
    sharers = lax.axis_size(PLANE_AXES)
    x = lax.all_to_all(snapshots, PAIR_AXES, 0, 0, tiled=True).reshape(PAIRS, rows, WIDE)
    keep, send, x = local_gram(x)
    part = (keep + swapped(send, "c", 1)).reshape(sharers, -1, WIDE)
    part = jnp.sum(lax.all_to_all(part, PLANE_AXES, 0, 0, tiled=True), axis=0)
    near, far, across = (swapped(part, "z", by) for by in (1, 2, 3))
    part = (part + near) + (far + across)
    part = part + swapped(part, "z", 6)
    part = jnp.broadcast_to(part[None], (sharers,) + part.shape)
    mine = lax.all_to_all(part, PLANE_AXES, 0, 0, tiled=True).reshape(SHARE, WIDE, WIDE)
    other = swapped(mine, "c", 1)
    y, norms = chain(mine, other, x)
    out = lax.all_to_all(y.reshape(snapshots.shape), PAIR_AXES, 0, 0, tiled=True)
    return out, norms.reshape(WIDE)


def solution(mesh):
    axes = ("yl", "z", "c", "x", "yh")
    finer = jax.sharding.Mesh(mesh.devices.reshape(2, 8, 2, 4, 2), axes)
    rows, pairs = ("yl", "z", "c"), PAIR_AXES
    return jax.shard_map(
        body,
        mesh=finer,
        in_specs=(P(rows, pairs),),
        out_specs=(P(rows, pairs), P(pairs)),
        check_vma=False,
    )
```
